512 devices in a mesh: group: 64 (over y, x, core), head: 8 (over z).
Axes of the slice: x: 4, y: 8, z: 8, core: 2. Of those that a mesh axis runs over, the one named last changes fastest.
Arguments:
- queries: bfloat16 [4096, 3072], P(('group', 'head')), may hold values from -9 to 9
- key_rows: bfloat16 [4096, 3072], P(('group', 'head')), may hold values from -6 to 6
- value_rows: bfloat16 [4096, 3072], P(('group', 'head')), may hold values from -6 to 6
- latent: float32 [4096, 3072], P(('group', 'head')), may hold values from -6 to 6
- fresh_noise: float32 [4096, 3072], P(('group', 'head')), may hold values from -6 to 6
- time_index: int32 [64], replicated, may hold values from 0 to 31
- lengths: int32 [64], replicated, may hold values from 1 to 64, 2560 in all
- visible: int32 [64, 64], replicated, may hold values 0 or 1
- time_gate: float32 [32, 3072], replicated, may hold values from 0.5 to 4
- step_size: float32 [32], replicated, may hold values from 0.25 to 1
- noise_level: float32 [32], replicated, may hold values from 0.1 to 0.5
Outputs:
- latent_next: float32 [4096, 3072], P(('group', 'head'))
The draws below stay inside these ranges and needn't reach their ends.
Inputs may be any that keep to these rules, and one draw needn't show every extreme that they name: `lengths`: some group is full.
All inputs are finite; a program needn't handle non-finite values.
Results may differ from the reference program's by a relative error of at most 0.0045.
Values may be sent and summed in bfloat16 or wider, within the bound.
No kernel may reach another device: no remote copies, remote signals or barrier semaphores. Data moves between devices by JAX's collectives and lax.ppermute only.
A program may use at most 64 MiB of HBM per device.

```python
import math
import jax
import jax.numpy as jnp
import numpy as np
from jax import lax

HEADS = 24
HD = 128
STEPS = 32
GROUPS = 64
GROUP_TOK = 64
TOKENS = 4096
FEAT = 3072


def draw_key_rows(key, part):
    key = jax.random.fold_in(key, 3)
    first_key = jax.random.fold_in(key, 0)
    shape = (TOKENS, HEADS * HD)
    base = jnp.clip(jax.random.normal(first_key, shape, jnp.float32), -5.0, 5.0)
    return base.astype(jnp.bfloat16)


def draw_queries(key, part):
    key = jax.random.fold_in(key, 7)
    first_key = jax.random.fold_in(key, 0)
    shape = (TOKENS, HEADS * HD)
    base = jnp.clip(jax.random.normal(first_key, shape, jnp.float32), -5.0, 5.0)
    return base.astype(jnp.bfloat16)


def place_ends(entries, own_key, least, largest):
    spot = [jax.random.randint(jax.random.fold_in(own_key, axis), (), 0, length) for axis, length in enumerate(entries.shape)]
    main_axis = entries.shape.index(max(entries.shape))
    neighbour = spot[:main_axis] + [(spot[main_axis] + 1) % entries.shape[main_axis]] + spot[main_axis + 1:]
    return entries.at[tuple(spot)].set(least).at[tuple(neighbour)].set(largest)


def block_scale(own_key, dims, pieces, smallest, top_value):
    gain, own = 1.0, jax.random.fold_in(own_key, 6)
    for dim, shards_of in pieces:
        draws = jnp.exp(jax.random.uniform(jax.random.fold_in(own, dim), (shards_of,), jnp.float32, smallest / len(pieces), top_value / len(pieces)))
        gain = gain * jnp.repeat(draws, dims[dim] // shards_of).reshape([-1 if axis == dim else 1 for axis in range(len(dims))])
    return gain


def split_up(count, total, reach, skew):
    weights = [(1 << 20) // math.isqrt(rank ** skew) + 1 for rank in range(2, count + 1)]
    rest, given = total - reach - (count - 1), [1] * (count - 1)
    while rest > 0:
        movable = [i for i in range(count - 1) if given[i] < reach]
        mass, left = sum([weights[i] for i in movable]), rest
        for i in movable:
            more = min(reach - given[i], max(1, left * weights[i] // mass), rest)
            given[i] = given[i] + more
            rest = rest - more
    return np.array([reach] + given)


def ragged(key, number_of, total, limit, slope):
    if number_of == 2:
        one = jax.random.randint(key, (), max(1, total - limit), min(limit, total - 1) + 1)
        return jnp.stack([one, total - one])
    sizes = jnp.asarray(split_up(number_of, total, limit, slope), jnp.int32)
    twos = (number_of - 1) // 2
    donor, receiver = sizes[1:1 + 2 * twos:2], sizes[2:2 + 2 * twos:2]
    room = jnp.minimum(donor - 1, limit - receiver)
    moved = jax.random.randint(jax.random.fold_in(key, 1), (twos,), 0, 1 << 20) % (room + 1)
    sizes = sizes.at[1:1 + 2 * twos:2].set(donor - moved).at[2:2 + 2 * twos:2].set(receiver + moved)
    return sizes[jax.random.permutation(jax.random.fold_in(key, 2), number_of)]


def gaussian(stream_key, extent, scale, most, pieces=(), held_as=jnp.bfloat16):
    values = jax.random.normal(stream_key, extent, jnp.float32) * scale
    if len(pieces) > 0:
        values = block_scale(stream_key, extent, pieces, -0.22, 0.18) * values
    return jnp.clip(values, min=-most, max=most).astype(held_as)


def setup_inputs(seed: int = 0) -> dict:
    key_list = jax.random.split(jax.random.key(seed), 12)
    return {
        "queries": draw_queries(jax.random.fold_in(key_list[11], 71), 0),
        "key_rows": draw_key_rows(jax.random.fold_in(key_list[11], 71), 0),
        "value_rows": gaussian(key_list[2], (TOKENS, FEAT), 1.0, 6.0, ((0, 512),)),
        "latent": gaussian(key_list[3], (TOKENS, FEAT), 1.0, 6.0, ((0, 512),), jnp.float32),
        "fresh_noise": gaussian(key_list[4], (TOKENS, FEAT), 1.0, 6.0, ((0, 512),), jnp.float32),
        "time_index": place_ends(jax.random.randint(key_list[5], (GROUPS,), 0, STEPS), jax.random.fold_in(key_list[5], 1), 0, STEPS - 1).astype(jnp.int32),
        "lengths": ragged(key_list[6], GROUPS, GROUPS * GROUP_TOK * 5 // 8, GROUP_TOK, 0).astype(jnp.int32),
        "visible": place_ends((jax.random.randint(key_list[7], (GROUPS, GROUPS), 0, 4) < 3).astype(jnp.int32), jax.random.fold_in(key_list[7], 1), 0, 1),
        "time_gate": jnp.clip(jnp.exp(jax.random.uniform(key_list[8], (STEPS, FEAT), jnp.float32, math.log(0.5), math.log(4.0))), 0.5, 4.0),
        "step_size": jnp.clip(jnp.exp(jax.random.uniform(key_list[9], (STEPS,), jnp.float32, math.log(0.25), math.log(1.0))), 0.25, 1.0),
        "noise_level": jnp.clip(jnp.exp(jax.random.uniform(key_list[10], (STEPS,), jnp.float32, math.log(0.1), math.log(0.5))), 0.1, 0.5),
    }


def reference(queries, key_rows, value_rows, latent, fresh_noise, time_index, lengths, visible, time_gate, step_size, noise_level):
    scale = HD ** -0.5
    position = jnp.arange(TOKENS).astype(jnp.int32)
    key_group = position // GROUP_TOK
    key_offset = position % GROUP_TOK
    key_live = key_offset < lengths[key_group]
    key_all = key_rows.astype(jnp.float32).reshape(TOKENS, HEADS, HD)
    value_all = value_rows.astype(jnp.float32).reshape(TOKENS, HEADS, HD)
    query_all = queries.reshape(GROUPS, GROUP_TOK, HEADS, HD)

    def attend_group(group):
        query_block = lax.dynamic_index_in_dim(query_all, group, 0, keepdims=False).astype(jnp.float32)
        scores = jnp.einsum("qhd,khd->hqk", query_block, key_all) * scale
        seen = visible[group][key_group] == 1
        allowed = ((key_group == group) | ((key_group < group) & seen)) & key_live
        scores = jnp.where(allowed[None, None, :], scores, -1e30)
        top = jnp.max(scores, axis=-1, keepdims=True)
        weights = jnp.where(allowed[None, None, :], jnp.exp(scores - top), 0.0)
        total = jnp.sum(weights, axis=-1)
        rounded = lax.optimization_barrier(weights.astype(jnp.bfloat16)).astype(jnp.float32)
        mixed = jnp.einsum("hqk,khd->qhd", rounded, value_all) / jnp.transpose(total)[:, :, None]
        return mixed.reshape(GROUP_TOK, HEADS * HD).astype(jnp.bfloat16)

    attention = lax.map(attend_group, jnp.arange(GROUPS).astype(jnp.int32))
    gate = time_gate[time_index]
    step_now = step_size[time_index]
    level_now = noise_level[time_index]
    live_rows = (jnp.arange(GROUP_TOK).astype(jnp.int32)[None, :] < lengths[:, None]).astype(jnp.float32)
    velocity = attention.astype(jnp.float32) * gate[:, None, :] * live_rows[:, :, None]
    result = latent.reshape(GROUPS, GROUP_TOK, HEADS * HD) + step_now[:, None, None] * velocity
    result = result + level_now[:, None, None] * fresh_noise.reshape(GROUPS, GROUP_TOK, HEADS * HD)
    return result.reshape(TOKENS, HEADS * HD)
```

```python
import functools

import jax
import jax.numpy as jnp
from jax import lax
from jax.experimental import pallas as pl
from jax.experimental.pallas import tpu as pltpu
from jax.sharding import Mesh
from jax.sharding import PartitionSpec as P

HD = 128
SLOTS = 64
GRID = 8
HEADS = 3
WIDE = HEADS * HD
LOW = -(2.0**100)
CHUNK = 4
LOG2E = 1.4426950408889634
LIMIT = pltpu.CompilerParams(vmem_limit_bytes=16 * 2**20)


def attend(q_ref, kv_ref, lengths_ref, visible_ref, out_ref):
    row = lax.axis_index("y")
    column = lax.axis_index("x") * 2 + lax.axis_index("core")
    keys = GRID * SLOTS
    lane = lax.broadcasted_iota(jnp.int32, (1, keys), 1)
    key_group = lane // SLOTS
    key_offset = lane - key_group * SLOTS
    alive = jnp.zeros((1, keys), jnp.int32)
    for j in range(GRID):
        alive = jnp.where(key_group == j, lengths_ref[row * GRID + j], alive)
    alive = key_offset < alive
    bias = []
    for i in range(GRID):
        own = i * GRID + column
        seen = jnp.zeros((1, keys), jnp.int32)
        for j in range(GRID):
            other = row * GRID + j
            flag = jnp.where(other < own, visible_ref[own, other], 0)
            flag = jnp.where(other == own, 1, flag)
            seen = jnp.where(key_group == j, flag, seen)
        bias.append(jnp.where((seen == 1) & alive, 0.0, LOW))
    spot = lax.broadcasted_iota(jnp.int32, (SLOTS, HD), 1)
    stats = [jnp.zeros((SLOTS, HD), jnp.float32)] * GRID
    ones = jnp.ones((keys, HD), jnp.bfloat16)
    for h in range(HEADS):
        part = slice(h * HD, (h + 1) * HD)
        values = jnp.concatenate([kv_ref[:, WIDE + h * HD : WIDE + (h + 1) * HD], ones], axis=1)
        for c in range(0, GRID, CHUNK):
            scores = lax.dot_general(
                q_ref[c : c + CHUNK, :, part].reshape(CHUNK * SLOTS, HD),
                kv_ref[:, part],
                (((1,), (1,)), ((), ())),
                preferred_element_type=jnp.float32,
            )
            raw, tops = [], []
            for i in range(CHUNK):
                score = scores[i * SLOTS : (i + 1) * SLOTS] * (HD**-0.5 * LOG2E) + bias[c + i]
                top = jnp.max(score, axis=1, keepdims=True)
                top = top.astype(jnp.bfloat16).astype(jnp.float32)
                raw.append(jnp.exp2(score - top).astype(jnp.bfloat16))
                tops.append(top)
            mixed = jnp.dot(
                jnp.concatenate(raw, axis=0), values, preferred_element_type=jnp.float32
            )
            for i in range(CHUNK):
                block = mixed[i * SLOTS : (i + 1) * SLOTS]
                out_ref[c + i, :, part] = block[:, :HD].astype(jnp.bfloat16)
                total = block[:, HD:]
                coarse = total.astype(jnp.bfloat16).astype(jnp.float32)
                stat = stats[c + i]
                stat = jnp.where(spot == h, tops[i], stat)
                stat = jnp.where(spot == h + 32, coarse, stat)
                stats[c + i] = jnp.where(spot == h + 64, total - coarse, stat)
    for i in range(GRID):
        out_ref[i, :, WIDE:] = stats[i].astype(jnp.bfloat16)


def update(time_ref, length_ref, step_ref, level_ref, part_ref, latent_ref, noise_ref, gate_ref, out_ref):
    group = (lax.axis_index("y") * 4 + lax.axis_index("x")) * 2 + lax.axis_index("core")
    now = time_ref[group]
    step = step_ref[now]
    level = level_ref[now]
    rows = latent_ref.shape[0]
    offset = lax.axis_index("head") * rows + lax.broadcasted_iota(jnp.int32, (rows, HD), 0)
    live = offset < length_ref[group]
    gate_rows = gate_ref[...]
    pick = lax.broadcasted_iota(jnp.int32, gate_rows.shape, 0) == now
    gate = jnp.sum(jnp.where(pick, gate_rows, 0.0), axis=0, keepdims=True)
    for g in range(GRID):
        stats = [part_ref[b * GRID + g, :, WIDE:].astype(jnp.float32) for b in range(GRID)]
        top = functools.reduce(jnp.maximum, stats)
        scale = [jnp.exp2(s - top) for s in stats]
        sums = [pltpu.roll(s, HD - 32, 1) + pltpu.roll(s, HD - 64, 1) for s in stats]
        total = functools.reduce(jnp.add, [w * s for w, s in zip(scale, sums)])
        for h in range(HEADS):
            part = slice(h * HD, (h + 1) * HD)
            mixed = functools.reduce(
                jnp.add,
                [
                    scale[b][:, h : h + 1] * part_ref[b * GRID + g, :, part].astype(jnp.float32)
                    for b in range(GRID)
                ],
            )
            mixed = mixed / total[:, h : h + 1]
            place = slice((g * HEADS + h) * HD, (g * HEADS + h + 1) * HD)
            velocity = jnp.where(live, mixed * gate[:, place], 0.0)
            out_ref[:, place] = (
                latent_ref[:, place] + step * velocity + level * noise_ref[:, place]
            )


def local(
    queries,
    key_rows,
    value_rows,
    latent,
    fresh_noise,
    time_index,
    lengths,
    visible,
    time_gate,
    step_size,
    noise_level,
):
    rows = queries.shape[0]
    vmem = pl.BlockSpec(memory_space=pltpu.VMEM)
    smem = pl.BlockSpec(memory_space=pltpu.SMEM)
    mine = jnp.concatenate(
        [a.reshape(rows, GRID, WIDE).swapaxes(0, 1) for a in (key_rows, value_rows, queries)],
        axis=2,
    )
    mine = lax.all_to_all(mine, "head", split_axis=0, concat_axis=0, tiled=True)
    mine = mine.reshape(SLOTS, 3 * WIDE)
    keys_values = lax.all_gather(mine[:, : 2 * WIDE], ("x", "core"), axis=0, tiled=True)
    head_queries = lax.all_to_all(
        jnp.broadcast_to(mine[None, :, 2 * WIDE :], (GRID, SLOTS, WIDE)),
        "y",
        split_axis=0,
        concat_axis=0,
        tiled=True,
    )
    partial = pl.pallas_call(
        attend,
        out_shape=jax.ShapeDtypeStruct((GRID, SLOTS, WIDE + HD), jnp.bfloat16),
        in_specs=[vmem, vmem, smem, smem],
        out_specs=vmem,
        compiler_params=LIMIT,
    )(head_queries, keys_values, lengths, visible)
    partial = lax.all_to_all(
        partial.reshape(GRID * GRID, rows, WIDE + HD),
        ("y", "head"),
        split_axis=0,
        concat_axis=0,
        tiled=True,
    )
    return pl.pallas_call(
        update,
        out_shape=jax.ShapeDtypeStruct(latent.shape, jnp.float32),
        in_specs=[smem] * 4 + [vmem] * 4,
        out_specs=vmem,
        compiler_params=LIMIT,
    )(time_index, lengths, step_size, noise_level, partial, latent, fresh_noise, time_gate)


def solution(mesh):
    grid = Mesh(mesh.devices.reshape(8, 4, 2, 8), ("y", "x", "core", "head"))
    tokens = P(("y", "x", "core", "head"), None)
    placed = (tokens,) * 5 + (P(),) * 6
    return jax.shard_map(local, mesh=grid, in_specs=placed, out_specs=tokens, check_vma=False)
```

```python
import functools

import jax
import jax.numpy as jnp
from jax import lax
from jax.experimental import pallas as pl
from jax.experimental.pallas import tpu as pltpu
from jax.sharding import Mesh
from jax.sharding import PartitionSpec as P

HD = 128
HEADS = 3
WIDE = HEADS * HD
SETS = 8
BANDS = 4
ROWS = 8
LOW = -(2.0**100)
LOG2E = 1.4426950408889634
LIMIT = pltpu.CompilerParams(vmem_limit_bytes=16 * 2**20)


def prepare(
    time_ref, length_ref, step_ref, level_ref, visible_ref, latent_ref, noise_ref, gate_ref,
    mine_ref, theirs_ref, base_ref, slope_ref,
):
    band = lax.axis_index("yh")
    core = lax.axis_index("core")
    blocks = BANDS * SETS
    keys = mine_ref.shape[1]
    groups = visible_ref.shape[0]
    lane = lax.broadcasted_iota(jnp.int32, (1, keys), 1)
    key_set = (lane // ROWS) % SETS
    key_offset = lane // (ROWS * SETS) * ROWS + lane % ROWS
    own = lax.broadcasted_iota(jnp.int32, (blocks, 1), 0) * 2 + core
    pick = own == lax.broadcasted_iota(jnp.int32, (blocks, groups), 1)
    rows = jnp.dot(
        pick.astype(jnp.bfloat16),
        visible_ref[...].astype(jnp.float32).astype(jnp.bfloat16),
        preferred_element_type=jnp.float32,
    ).astype(jnp.bfloat16)
    for key_core, bias_ref in ((core, mine_ref), (1 - core, theirs_ref)):
        key_group = band * (2 * SETS) + key_set * 2 + key_core
        length = jnp.zeros((1, keys), jnp.int32)
        for j in range(SETS):
            length = jnp.where(
                key_set == j, length_ref[band * (2 * SETS) + 2 * j + key_core], length
            )
        spread = lax.broadcasted_iota(jnp.int32, (groups, keys), 0) == key_group
        seen = jnp.dot(rows, spread.astype(jnp.bfloat16), preferred_element_type=jnp.float32)
        reach = (key_group == own) | ((key_group < own) & (seen > 0.5))
        bias = jnp.where(reach & (key_offset < length), 0.0, LOW)
        for j in range(blocks):
            bias_ref[j * ROWS : (j + 1) * ROWS, :] = jnp.broadcast_to(bias[j : j + 1], (ROWS, keys))
    group = band * 2 + lax.axis_index("yl")
    group = (group * 4 + lax.axis_index("x")) * 2 + core
    now = time_ref[group]
    offset = lax.axis_index("head") * ROWS + lax.broadcasted_iota(jnp.int32, latent_ref.shape, 0)
    pick = lax.broadcasted_iota(jnp.int32, gate_ref.shape, 0) == now
    gate = jnp.sum(jnp.where(pick, gate_ref[...], 0.0), axis=0, keepdims=True)
    slope_ref[...] = jnp.where(offset < length_ref[group], step_ref[now] * gate, 0.0)
    base_ref[...] = latent_ref[...] + level_ref[now] * noise_ref[...]


def attend(q_ref, first_ref, second_ref, *refs):
    *bias_refs, out_ref = refs
    key_refs = (first_ref, second_ref)
    queries, keys = q_ref.shape[0], first_ref.shape[0]
    spot = lax.broadcasted_iota(jnp.int32, (queries, HD), 1)
    stat = jnp.zeros((queries, HD), jnp.float32)
    ones = jnp.ones((keys, HD), jnp.bfloat16)
    for h in range(HEADS):
        part = slice(h * HD, (h + 1) * HD)
        scores = []
        for key_ref, bias_ref in zip(key_refs, bias_refs):
            score = lax.dot_general(
                q_ref[:, part],
                key_ref[:, part],
                (((1,), (1,)), ((), ())),
                preferred_element_type=jnp.float32,
            )
            scores.append(score * (HD**-0.5 * LOG2E) + bias_ref[...])
        top = jnp.max(functools.reduce(jnp.maximum, scores), axis=1, keepdims=True)
        top = top.astype(jnp.bfloat16).astype(jnp.float32)
        mixed = jnp.zeros((queries, 2 * HD), jnp.float32)
        for score, key_ref in zip(scores, key_refs):
            values = key_ref[:, WIDE + h * HD : WIDE + (h + 1) * HD]
            mixed += jnp.dot(
                jnp.exp2(score - top).astype(jnp.bfloat16),
                jnp.concatenate([values, ones], axis=1),
                preferred_element_type=jnp.float32,
            )
        out_ref[:, part] = mixed[:, :HD].astype(jnp.bfloat16)
        total = mixed[:, HD:]
        coarse = total.astype(jnp.bfloat16).astype(jnp.float32)
        stat = jnp.where(spot == h, top, stat)
        stat = jnp.where(spot == h + 32, coarse, stat)
        stat = jnp.where(spot == h + 64, total - coarse, stat)
    out_ref[:, WIDE:] = stat.astype(jnp.bfloat16)


def update(part_ref, base_ref, slope_ref, out_ref):
    for g in range(SETS):
        stats = [part_ref[b * SETS + g, :, WIDE:].astype(jnp.float32) for b in range(BANDS)]
        top = functools.reduce(jnp.maximum, stats)
        scale = [jnp.exp2(s - top) for s in stats]
        sums = [pltpu.roll(s, HD - 32, 1) + pltpu.roll(s, HD - 64, 1) for s in stats]
        total = functools.reduce(jnp.add, [w * s for w, s in zip(scale, sums)])
        scale = [w / total for w in scale]
        for h in range(HEADS):
            part = slice(h * HD, (h + 1) * HD)
            mixed = functools.reduce(
                jnp.add,
                [
                    scale[b][:, h : h + 1] * part_ref[b * SETS + g, :, part].astype(jnp.float32)
                    for b in range(BANDS)
                ],
            )
            place = slice((g * HEADS + h) * HD, (g * HEADS + h + 1) * HD)
            out_ref[:, place] = base_ref[:, place] + slope_ref[:, place] * mixed


def local(
    queries,
    key_rows,
    value_rows,
    latent,
    fresh_noise,
    time_index,
    lengths,
    visible,
    time_gate,
    step_size,
    noise_level,
):
    vmem = pl.BlockSpec(memory_space=pltpu.VMEM)
    smem = pl.BlockSpec(memory_space=pltpu.SMEM)
    mine = jnp.concatenate(
        [a.reshape(ROWS, SETS, WIDE).swapaxes(0, 1) for a in (key_rows, value_rows, queries)],
        axis=2,
    )
    mine = lax.all_to_all(mine, ("yl", "x"), split_axis=0, concat_axis=0, tiled=True)
    mine = mine.reshape(SETS * ROWS, 3 * WIDE)
    slices = lax.all_to_all(
        jnp.broadcast_to(mine[None, :, : 2 * WIDE], (SETS, SETS * ROWS, 2 * WIDE)),
        "head",
        split_axis=0,
        concat_axis=0,
        tiled=True,
    )
    head_queries = lax.all_gather(mine[:, 2 * WIDE :], "yh", axis=0, tiled=True)
    slices, head_queries = lax.optimization_barrier((slices, head_queries))
    slices = slices.reshape(-1, 2 * WIDE)
    halves = [slices, lax.ppermute(slices, "core", [(0, 1), (1, 0)])]
    rows, keys = BANDS * SETS * ROWS, SETS * SETS * ROWS
    bias = jax.ShapeDtypeStruct((rows, keys), jnp.float32)
    *biases, base, slope = pl.pallas_call(
        prepare,
        out_shape=[bias, bias] + [jax.ShapeDtypeStruct(latent.shape, jnp.float32)] * 2,
        in_specs=[smem] * 4 + [vmem] * 4,
        out_specs=[vmem] * 4,
        compiler_params=LIMIT,
        cost_estimate=pl.CostEstimate(flops=10**8, bytes_accessed=2**21, transcendentals=0),
    )(time_index, lengths, step_size, noise_level, visible, latent, fresh_noise, time_gate)
    partial = pl.pallas_call(
        attend,
        out_shape=jax.ShapeDtypeStruct((rows, WIDE + HD), jnp.bfloat16),
        in_specs=[vmem] * 5,
        out_specs=vmem,
        compiler_params=LIMIT,
    )(head_queries, *halves, *biases)
    partial = lax.all_to_all(
        partial.reshape(BANDS * SETS, ROWS, WIDE + HD),
        ("yh", "yl", "x"),
        split_axis=0,
        concat_axis=0,
        tiled=True,
    )
    return pl.pallas_call(
        update,
        out_shape=jax.ShapeDtypeStruct(latent.shape, jnp.float32),
        in_specs=[vmem] * 3,
        out_specs=vmem,
        compiler_params=LIMIT,
    )(partial, base, slope)


def solution(mesh):
    names = ("yh", "yl", "x", "core", "head")
    grid = Mesh(mesh.devices.reshape(BANDS, 2, 4, 2, 8), names)
    tokens = P(names, None)
    placed = (tokens,) * 5 + (P(),) * 6
    return jax.shard_map(local, mesh=grid, in_specs=placed, out_specs=tokens, check_vma=False)
```

```python
import functools

import jax
import jax.numpy as jnp
from jax import lax
from jax.experimental import pallas as pl
from jax.experimental.pallas import tpu as pltpu
from jax.sharding import Mesh
from jax.sharding import PartitionSpec as P

HD = 128
HEADS = 3
WIDE = HEADS * HD
SETS = 8
BANDS = 4
ORDER = (0, 1, 3, 2)
ROWS = 8
SLOTS = 64
SWAP = [(0, 1), (1, 0)]
LOW = -(2.0**100)
LOG2E = 1.4426950408889634
LIMIT = pltpu.CompilerParams(vmem_limit_bytes=16 * 2**20)


def prepare(
    time_ref, length_ref, step_ref, level_ref, visible_ref, latent_ref, noise_ref, gate_ref,
    bias_ref, base_ref, slope_ref,
):
    band = lax.axis_index("yh")
    core = lax.axis_index("core")
    column = lax.axis_index("yl") * 8 + lax.axis_index("x") * 2 + core
    keys = bias_ref.shape[1]
    groups = visible_ref.shape[0]
    lane = lax.broadcasted_iota(jnp.int32, (1, keys), 1)
    key_set = lane // SLOTS
    key_offset = lane - key_set * SLOTS
    shift = lax.broadcasted_iota(jnp.int32, (BANDS, 1), 0)
    shift = jnp.where(shift < 2, shift, BANDS + 1 - shift)
    own = lax.rem(band + BANDS - shift, BANDS) * (2 * SETS) + column
    pick = own == lax.broadcasted_iota(jnp.int32, (BANDS, groups), 1)
    rows = jnp.dot(
        pick.astype(jnp.bfloat16),
        visible_ref[...].astype(jnp.float32).astype(jnp.bfloat16),
        preferred_element_type=jnp.float32,
    ).astype(jnp.bfloat16)
    for half, key_core in enumerate((core, 1 - core)):
        key_group = band * (2 * SETS) + key_set * 2 + key_core
        length = jnp.zeros((1, keys), jnp.int32)
        for j in range(SETS):
            length = jnp.where(
                key_set == j, length_ref[band * (2 * SETS) + 2 * j + key_core], length
            )
        spread = lax.broadcasted_iota(jnp.int32, (groups, keys), 0) == key_group
        seen = jnp.dot(rows, spread.astype(jnp.bfloat16), preferred_element_type=jnp.float32)
        reach = (key_group == own) | ((key_group < own) & (seen > 0.5))
        bias = jnp.where(reach & (key_offset < length), 0.0, LOW)
        bias_ref[half * BANDS : (half + 1) * BANDS, :] = bias
    group = band * 2 + lax.axis_index("yl")
    group = (group * 4 + lax.axis_index("x")) * 2 + core
    now = time_ref[group]
    offset = lax.axis_index("head") * ROWS + lax.broadcasted_iota(jnp.int32, latent_ref.shape, 0)
    pick = lax.broadcasted_iota(jnp.int32, gate_ref.shape, 0) == now
    gate = jnp.sum(jnp.where(pick, gate_ref[...], 0.0), axis=0, keepdims=True)
    slope_ref[...] = jnp.where(offset < length_ref[group], step_ref[now] * gate, 0.0)
    base_ref[...] = latent_ref[...] + level_ref[now] * noise_ref[...]


def attend(*refs):
    query_refs, key_refs = refs[:BANDS], refs[BANDS : BANDS + 2]
    bias_ref, out_ref = refs[BANDS + 2 :]
    band = lax.axis_index("yh")
    bands = [lax.rem(band + BANDS - k, BANDS) for k in ORDER]
    keys = key_refs[0].shape[0]
    spot = lax.broadcasted_iota(jnp.int32, (SLOTS, HD), 1)
    stats = [jnp.zeros((SLOTS, HD), jnp.float32)] * BANDS
    ones = jnp.ones((keys, HD), jnp.bfloat16)
    for h in range(HEADS):
        part = slice(h * HD, (h + 1) * HD)
        query = jnp.concatenate([q[:, part] for q in query_refs], axis=0)
        scores = [
            lax.dot_general(
                query, key[:, part], (((1,), (1,)), ((), ())), preferred_element_type=jnp.float32
            )
            for key in key_refs
        ]
        raws, tops = ([], []), []
        for k in range(BANDS):
            place = slice(k * SLOTS, (k + 1) * SLOTS)
            score = [
                s[place] * (HD**-0.5 * LOG2E) + bias_ref[half * BANDS + k : half * BANDS + k + 1, :]
                for half, s in enumerate(scores)
            ]
            top = jnp.max(jnp.maximum(*score), axis=1, keepdims=True)
            top = top.astype(jnp.bfloat16).astype(jnp.float32)
            tops.append(top)
            for raw, s in zip(raws, score):
                raw.append(jnp.exp2(s - top).astype(jnp.bfloat16))
        mixed = jnp.zeros((BANDS * SLOTS, 2 * HD), jnp.float32)
        for raw, key in zip(raws, key_refs):
            values = jnp.concatenate([key[:, WIDE + h * HD : WIDE + (h + 1) * HD], ones], axis=1)
            mixed += jnp.dot(
                jnp.concatenate(raw, axis=0), values, preferred_element_type=jnp.float32
            )
        for k in range(BANDS):
            block = mixed[k * SLOTS : (k + 1) * SLOTS]
            out_ref[bands[k], :, part] = block[:, :HD].astype(jnp.bfloat16)
            total = block[:, HD:]
            coarse = total.astype(jnp.bfloat16).astype(jnp.float32)
            stat = stats[k]
            stat = jnp.where(spot == h, tops[k], stat)
            stat = jnp.where(spot == h + 32, coarse, stat)
            stats[k] = jnp.where(spot == h + 64, total - coarse, stat)
    for k in range(BANDS):
        out_ref[bands[k], :, WIDE:] = stats[k].astype(jnp.bfloat16)


def update(part_ref, base_ref, slope_ref, out_ref):
    for g in range(SETS):
        stats = [part_ref[b * SETS + g, :, WIDE:].astype(jnp.float32) for b in range(BANDS)]
        top = functools.reduce(jnp.maximum, stats)
        scale = [jnp.exp2(s - top) for s in stats]
        sums = [pltpu.roll(s, HD - 32, 1) + pltpu.roll(s, HD - 64, 1) for s in stats]
        total = functools.reduce(jnp.add, [w * s for w, s in zip(scale, sums)])
        scale = [w / total for w in scale]
        for h in range(HEADS):
            part = slice(h * HD, (h + 1) * HD)
            mixed = functools.reduce(
                jnp.add,
                [
                    scale[b][:, h : h + 1] * part_ref[b * SETS + g, :, part].astype(jnp.float32)
                    for b in range(BANDS)
                ],
            )
            place = slice((g * HEADS + h) * HD, (g * HEADS + h + 1) * HD)
            out_ref[:, place] = base_ref[:, place] + slope_ref[:, place] * mixed


def local(
    queries,
    key_rows,
    value_rows,
    latent,
    fresh_noise,
    time_index,
    lengths,
    visible,
    time_gate,
    step_size,
    noise_level,
):
    vmem = pl.BlockSpec(memory_space=pltpu.VMEM)
    smem = pl.BlockSpec(memory_space=pltpu.SMEM)
    mine = jnp.concatenate(
        [a.reshape(ROWS, SETS, WIDE).swapaxes(0, 1) for a in (key_rows, value_rows, queries)],
        axis=2,
    )
    mine = lax.all_to_all(mine, "head", split_axis=0, concat_axis=0, tiled=True)
    mine = mine.reshape(SLOTS, 3 * WIDE)
    query = mine[:, 2 * WIDE :]
    own = lax.all_to_all(
        jnp.broadcast_to(mine[None, :, : 2 * WIDE], (SETS, SLOTS, 2 * WIDE)),
        ("yl", "x"),
        split_axis=0,
        concat_axis=0,
        tiled=True,
    ).reshape(SETS * SLOTS, 2 * WIDE)
    sent = [
        lax.ppermute(query, "yh", [(i, (i + k) % BANDS) for i in range(BANDS)])
        for k in ORDER[1:]
    ]
    bias = jax.ShapeDtypeStruct((2 * BANDS, SETS * SLOTS), jnp.float32)
    prepared = pl.pallas_call(
        prepare,
        out_shape=[bias] + [jax.ShapeDtypeStruct(latent.shape, jnp.float32)] * 2,
        in_specs=[smem] * 4 + [vmem] * 4,
        out_specs=[vmem] * 3,
        compiler_params=LIMIT,
    )(time_index, lengths, step_size, noise_level, visible, latent, fresh_noise, time_gate)
    own, sent = lax.optimization_barrier((own, sent))
    bias, base, slope = prepared
    other = lax.ppermute(own, "core", SWAP)
    partial = pl.pallas_call(
        attend,
        out_shape=jax.ShapeDtypeStruct((BANDS, SLOTS, WIDE + HD), jnp.bfloat16),
        in_specs=[vmem] * (BANDS + 3),
        out_specs=vmem,
        compiler_params=LIMIT,
    )(query, *sent, own, other, bias)
    partial = lax.all_to_all(
        partial.reshape(BANDS * SETS, ROWS, WIDE + HD),
        ("yh", "head"),
        split_axis=0,
        concat_axis=0,
        tiled=True,
    )
    return pl.pallas_call(
        update,
        out_shape=jax.ShapeDtypeStruct(latent.shape, jnp.float32),
        in_specs=[vmem] * 3,
        out_specs=vmem,
        compiler_params=LIMIT,
    )(partial, base, slope)


def solution(mesh):
    names = ("yh", "yl", "x", "core", "head")
    grid = Mesh(mesh.devices.reshape(BANDS, 2, 4, 2, 8), names)
    tokens = P(names, None)
    placed = (tokens,) * 5 + (P(),) * 6
    return jax.shard_map(local, mesh=grid, in_specs=placed, out_specs=tokens, check_vma=False)
```

```python
import functools

import jax
import jax.numpy as jnp
from jax import lax
from jax.experimental import pallas as pl
from jax.experimental.pallas import tpu as pltpu
from jax.sharding import Mesh
from jax.sharding import PartitionSpec as P

HD = 128
HEADS = 3
WIDE = HEADS * HD
SETS = 8
BANDS = 4
ORDER = (0, 2, 1, 3)
ROWS = 8
SLOTS = 64
SWAP = [(0, 1), (1, 0)]
LOW = -(2.0**100)
LOG2E = 1.4426950408889634
LIMIT = pltpu.CompilerParams(vmem_limit_bytes=16 * 2**20)


def prepare(
    time_ref, length_ref, step_ref, level_ref, visible_ref, latent_ref, noise_ref, gate_ref,
    bias_ref, base_ref, slope_ref,
):
    band = lax.axis_index("yh")
    core = lax.axis_index("core")
    column = lax.axis_index("yl") * 8 + lax.axis_index("x") * 2 + core
    keys = bias_ref.shape[1]
    groups = visible_ref.shape[0]
    lane = lax.broadcasted_iota(jnp.int32, (1, keys), 1)
    key_set = lane // SLOTS
    key_offset = lane - key_set * SLOTS
    shift = lax.broadcasted_iota(jnp.int32, (BANDS, 1), 0)
    shift = sum(jnp.where(shift == k, ORDER[k], 0) for k in range(BANDS))
    own = lax.rem(band + BANDS - shift, BANDS) * (2 * SETS) + column
    pick = own == lax.broadcasted_iota(jnp.int32, (BANDS, groups), 1)
    rows = jnp.dot(
        pick.astype(jnp.bfloat16),
        visible_ref[...].astype(jnp.float32).astype(jnp.bfloat16),
        preferred_element_type=jnp.float32,
    ).astype(jnp.bfloat16)
    for half in range(2):
        local_group = (lane // SLOTS % BANDS + half * BANDS) * 2 + lane // (SLOTS * BANDS)
        key_group = band * (2 * SETS) + local_group
        length = jnp.zeros((1, keys), jnp.int32)
        for j in range(SETS):
            local = half * SETS + j
            length = jnp.where(
                local_group == local, length_ref[band * (2 * SETS) + local], length
            )
        spread = lax.broadcasted_iota(jnp.int32, (groups, keys), 0) == key_group
        seen = jnp.dot(rows, spread.astype(jnp.bfloat16), preferred_element_type=jnp.float32)
        reach = (key_group == own) | ((key_group < own) & (seen > 0.5))
        bias = jnp.where(reach & (key_offset < length), 0.0, LOW)
        bias_ref[half * BANDS : (half + 1) * BANDS, :] = bias
    group = band * 2 + lax.axis_index("yl")
    group = (group * 4 + lax.axis_index("x")) * 2 + core
    now = time_ref[group]
    offset = lax.axis_index("head") * ROWS + lax.broadcasted_iota(jnp.int32, latent_ref.shape, 0)
    pick = lax.broadcasted_iota(jnp.int32, gate_ref.shape, 0) == now
    gate = jnp.sum(jnp.where(pick, gate_ref[...], 0.0), axis=0, keepdims=True)
    slope_ref[...] = jnp.where(offset < length_ref[group], step_ref[now] * gate, 0.0)
    base_ref[...] = latent_ref[...] + level_ref[now] * noise_ref[...]


def attend(*refs):
    query_refs, key_refs = refs[:BANDS], refs[BANDS : BANDS + 2]
    bias_ref, out_ref = refs[BANDS + 2 :]
    band = lax.axis_index("yh")
    bands = [lax.rem(band + BANDS - k, BANDS) for k in ORDER]
    keys = key_refs[0].shape[0]
    spot = lax.broadcasted_iota(jnp.int32, (SLOTS, HD), 1)
    stats = [jnp.zeros((SLOTS, HD), jnp.float32)] * BANDS
    ones = jnp.ones((keys, HD), jnp.bfloat16)
    for h in range(HEADS):
        part = slice(h * HD, (h + 1) * HD)
        query = jnp.concatenate([q[:, part] for q in query_refs], axis=0)
        scores = [
            lax.dot_general(
                query, key[:, part], (((1,), (1,)), ((), ())), preferred_element_type=jnp.float32
            )
            for key in key_refs
        ]
        raws, tops = ([], []), []
        for k in range(BANDS):
            place = slice(k * SLOTS, (k + 1) * SLOTS)
            score = [
                s[place] * (HD**-0.5 * LOG2E) + bias_ref[half * BANDS + k : half * BANDS + k + 1, :]
                for half, s in enumerate(scores)
            ]
            top = jnp.max(jnp.maximum(*score), axis=1, keepdims=True)
            top = top.astype(jnp.bfloat16).astype(jnp.float32)
            tops.append(top)
            for raw, s in zip(raws, score):
                raw.append(jnp.exp2(s - top).astype(jnp.bfloat16))
        mixed = jnp.zeros((BANDS * SLOTS, 2 * HD), jnp.float32)
        for raw, key in zip(raws, key_refs):
            values = jnp.concatenate([key[:, WIDE + h * HD : WIDE + (h + 1) * HD], ones], axis=1)
            mixed += jnp.dot(
                jnp.concatenate(raw, axis=0), values, preferred_element_type=jnp.float32
            )
        for k in range(BANDS):
            block = mixed[k * SLOTS : (k + 1) * SLOTS]
            out_ref[bands[k], :, part] = block[:, :HD].astype(jnp.bfloat16)
            total = block[:, HD:]
            coarse = total.astype(jnp.bfloat16).astype(jnp.float32)
            stat = stats[k]
            stat = jnp.where(spot == h, tops[k], stat)
            stat = jnp.where(spot == h + 32, coarse, stat)
            stats[k] = jnp.where(spot == h + 64, total - coarse, stat)
    for k in range(BANDS):
        out_ref[bands[k], :, WIDE:] = stats[k].astype(jnp.bfloat16)


def update(part_ref, base_ref, slope_ref, out_ref):
    for g in range(SETS):
        stats = [part_ref[b * SETS + g, :, WIDE:].astype(jnp.float32) for b in range(BANDS)]
        top = functools.reduce(jnp.maximum, stats)
        scale = [jnp.exp2(s - top) for s in stats]
        sums = [pltpu.roll(s, HD - 32, 1) + pltpu.roll(s, HD - 64, 1) for s in stats]
        total = functools.reduce(jnp.add, [w * s for w, s in zip(scale, sums)])
        scale = [w / total for w in scale]
        for h in range(HEADS):
            part = slice(h * HD, (h + 1) * HD)
            mixed = functools.reduce(
                jnp.add,
                [
                    scale[b][:, h : h + 1] * part_ref[b * SETS + g, :, part].astype(jnp.float32)
                    for b in range(BANDS)
                ],
            )
            place = slice((g * HEADS + h) * HD, (g * HEADS + h + 1) * HD)
            out_ref[:, place] = base_ref[:, place] + slope_ref[:, place] * mixed


def local(
    queries,
    key_rows,
    value_rows,
    latent,
    fresh_noise,
    time_index,
    lengths,
    visible,
    time_gate,
    step_size,
    noise_level,
):
    vmem = pl.BlockSpec(memory_space=pltpu.VMEM)
    smem = pl.BlockSpec(memory_space=pltpu.SMEM)
    mine = jnp.concatenate(
        [a.reshape(ROWS, SETS, WIDE).swapaxes(0, 1) for a in (key_rows, value_rows, queries)],
        axis=2,
    )
    mine = lax.all_to_all(mine, "head", split_axis=0, concat_axis=0, tiled=True)
    mine = mine.reshape(SLOTS, 3 * WIDE)
    query = mine[:, 2 * WIDE :]
    own = lax.all_to_all(
        jnp.broadcast_to(mine[None, :, : 2 * WIDE], (SETS, SLOTS, 2 * WIDE)),
        ("yl", "x"),
        split_axis=0,
        concat_axis=0,
        tiled=True,
    )
    sent = [
        lax.ppermute(query, "yh", [(i, (i + k) % BANDS) for i in range(BANDS)])
        for k in ORDER[1:]
    ]
    bias = jax.ShapeDtypeStruct((2 * BANDS, SETS * SLOTS), jnp.float32)
    prepared = pl.pallas_call(
        prepare,
        out_shape=[bias] + [jax.ShapeDtypeStruct(latent.shape, jnp.float32)] * 2,
        in_specs=[smem] * 4 + [vmem] * 4,
        out_specs=[vmem] * 3,
        compiler_params=LIMIT,
    )(time_index, lengths, step_size, noise_level, visible, latent, fresh_noise, time_gate)
    bias, base, slope = prepared
    halves = [
        lax.all_gather(a.reshape(-1, 2 * WIDE), "core", axis=0, tiled=True)
        for a in (own[:BANDS], own[BANDS:])
    ]
    partial = pl.pallas_call(
        attend,
        out_shape=jax.ShapeDtypeStruct((BANDS, SLOTS, WIDE + HD), jnp.bfloat16),
        in_specs=[vmem] * (BANDS + 3),
        out_specs=vmem,
        compiler_params=LIMIT,
    )(query, *sent, *halves, bias)
    partial = lax.all_to_all(
        partial.reshape(BANDS * SETS, ROWS, WIDE + HD),
        ("yh", "head"),
        split_axis=0,
        concat_axis=0,
        tiled=True,
    )
    return pl.pallas_call(
        update,
        out_shape=jax.ShapeDtypeStruct(latent.shape, jnp.float32),
        in_specs=[vmem] * 3,
        out_specs=vmem,
        compiler_params=LIMIT,
    )(partial, base, slope)


def solution(mesh):
    names = ("yh", "yl", "x", "core", "head")
    grid = Mesh(mesh.devices.reshape(BANDS, 2, 4, 2, 8), names)
    tokens = P(names, None)
    placed = (tokens,) * 5 + (P(),) * 6
    return jax.shard_map(local, mesh=grid, in_specs=placed, out_specs=tokens, check_vma=False)
```

```python
import functools

import jax
import jax.numpy as jnp
from jax import lax
from jax.experimental import pallas as pl
from jax.experimental.pallas import tpu as pltpu
from jax.sharding import Mesh
from jax.sharding import PartitionSpec as P

HD = 128
HEADS = 3
WIDE = HEADS * HD
SETS = 8
BANDS = 4
ORDER = (0, 2, 1, 3)
ROWS = 8
SLOTS = 64
SWAP = [(0, 1), (1, 0)]
LOW = -(2.0**100)
LOG2E = 1.4426950408889634
LIMIT = pltpu.CompilerParams(vmem_limit_bytes=16 * 2**20)


def prepare(
    time_ref, length_ref, step_ref, level_ref, visible_ref, latent_ref, noise_ref, gate_ref,
    bias_ref, base_ref, slope_ref,
):
    band = lax.axis_index("yh")
    core = lax.axis_index("core")
    column = lax.axis_index("yl") * 8 + lax.axis_index("x") * 2 + core
    keys = bias_ref.shape[1]
    groups = visible_ref.shape[0]
    lane = lax.broadcasted_iota(jnp.int32, (1, keys), 1)
    key_set = lane // SLOTS
    key_offset = lane - key_set * SLOTS
    shift = lax.broadcasted_iota(jnp.int32, (BANDS, 1), 0)
    shift = sum(jnp.where(shift == k, ORDER[k], 0) for k in range(BANDS))
    own = lax.rem(band + BANDS - shift, BANDS) * (2 * SETS) + column
    pick = own == lax.broadcasted_iota(jnp.int32, (BANDS, groups), 1)
    rows = jnp.dot(
        pick.astype(jnp.bfloat16),
        visible_ref[...].astype(jnp.float32).astype(jnp.bfloat16),
        preferred_element_type=jnp.float32,
    ).astype(jnp.bfloat16)
    for half in range(2):
        key_set = lane // SLOTS % BANDS + half * BANDS
        local_group = key_set % 2 * SETS + key_set // 2 * 2 + lane // (SLOTS * BANDS)
        key_group = band * (2 * SETS) + local_group
        length = jnp.zeros((1, keys), jnp.int32)
        for side in range(2):
            for j in range(BANDS):
                local = side * SETS + half * BANDS + j
                length = jnp.where(
                    local_group == local, length_ref[band * (2 * SETS) + local], length
                )
        spread = lax.broadcasted_iota(jnp.int32, (groups, keys), 0) == key_group
        seen = jnp.dot(rows, spread.astype(jnp.bfloat16), preferred_element_type=jnp.float32)
        reach = (key_group == own) | ((key_group < own) & (seen > 0.5))
        bias = jnp.where(reach & (key_offset < length), 0.0, LOW)
        bias_ref[half * BANDS : (half + 1) * BANDS, :] = bias
    group = band * 2 + lax.axis_index("yl")
    group = (group * 4 + lax.axis_index("x")) * 2 + core
    now = time_ref[group]
    offset = lax.axis_index("head") * ROWS + lax.broadcasted_iota(jnp.int32, latent_ref.shape, 0)
    pick = lax.broadcasted_iota(jnp.int32, gate_ref.shape, 0) == now
    gate = jnp.sum(jnp.where(pick, gate_ref[...], 0.0), axis=0, keepdims=True)
    slope_ref[...] = jnp.where(offset < length_ref[group], step_ref[now] * gate, 0.0)
    base_ref[...] = latent_ref[...] + level_ref[now] * noise_ref[...]


def attend(*refs):
    query_refs, key_refs = refs[:BANDS], refs[BANDS : BANDS + 2]
    bias_ref, out_ref = refs[BANDS + 2 :]
    band = lax.axis_index("yh")
    bands = [lax.rem(band + BANDS - k, BANDS) for k in ORDER]
    keys = key_refs[0].shape[0]
    spot = lax.broadcasted_iota(jnp.int32, (SLOTS, HD), 1)
    stats = [jnp.zeros((SLOTS, HD), jnp.float32)] * BANDS
    ones = jnp.ones((keys, HD), jnp.bfloat16)
    for h in range(HEADS):
        part = slice(h * HD, (h + 1) * HD)
        query = jnp.concatenate([q[:, part] for q in query_refs], axis=0)
        scores = [
            lax.dot_general(
                query, key[:, part], (((1,), (1,)), ((), ())), preferred_element_type=jnp.float32
            )
            for key in key_refs
        ]
        raws, tops = ([], []), []
        for k in range(BANDS):
            place = slice(k * SLOTS, (k + 1) * SLOTS)
            score = [
                s[place] * (HD**-0.5 * LOG2E) + bias_ref[half * BANDS + k : half * BANDS + k + 1, :]
                for half, s in enumerate(scores)
            ]
            top = jnp.max(jnp.maximum(*score), axis=1, keepdims=True)
            top = top.astype(jnp.bfloat16).astype(jnp.float32)
            tops.append(top)
            for raw, s in zip(raws, score):
                raw.append(jnp.exp2(s - top).astype(jnp.bfloat16))
        mixed = jnp.zeros((BANDS * SLOTS, 2 * HD), jnp.float32)
        for raw, key in zip(raws, key_refs):
            values = jnp.concatenate([key[:, WIDE + h * HD : WIDE + (h + 1) * HD], ones], axis=1)
            mixed += jnp.dot(
                jnp.concatenate(raw, axis=0), values, preferred_element_type=jnp.float32
            )
        for k in range(BANDS):
            block = mixed[k * SLOTS : (k + 1) * SLOTS]
            out_ref[bands[k], :, part] = block[:, :HD].astype(jnp.bfloat16)
            total = block[:, HD:]
            coarse = total.astype(jnp.bfloat16).astype(jnp.float32)
            stat = stats[k]
            stat = jnp.where(spot == h, tops[k], stat)
            stat = jnp.where(spot == h + 32, coarse, stat)
            stats[k] = jnp.where(spot == h + 64, total - coarse, stat)
    for k in range(BANDS):
        out_ref[bands[k], :, WIDE:] = stats[k].astype(jnp.bfloat16)


def update(part_ref, base_ref, slope_ref, out_ref):
    for g in range(SETS):
        stats = [part_ref[b * SETS + g, :, WIDE:].astype(jnp.float32) for b in range(BANDS)]
        top = functools.reduce(jnp.maximum, stats)
        scale = [jnp.exp2(s - top) for s in stats]
        sums = [pltpu.roll(s, HD - 32, 1) + pltpu.roll(s, HD - 64, 1) for s in stats]
        total = functools.reduce(jnp.add, [w * s for w, s in zip(scale, sums)])
        scale = [w / total for w in scale]
        for h in range(HEADS):
            part = slice(h * HD, (h + 1) * HD)
            mixed = functools.reduce(
                jnp.add,
                [
                    scale[b][:, h : h + 1] * part_ref[b * SETS + g, :, part].astype(jnp.float32)
                    for b in range(BANDS)
                ],
            )
            place = slice((g * HEADS + h) * HD, (g * HEADS + h + 1) * HD)
            out_ref[:, place] = base_ref[:, place] + slope_ref[:, place] * mixed


def local(
    queries,
    key_rows,
    value_rows,
    latent,
    fresh_noise,
    time_index,
    lengths,
    visible,
    time_gate,
    step_size,
    noise_level,
):
    vmem = pl.BlockSpec(memory_space=pltpu.VMEM)
    smem = pl.BlockSpec(memory_space=pltpu.SMEM)
    mine = jnp.concatenate(
        [a.reshape(ROWS, SETS, WIDE).swapaxes(0, 1) for a in (key_rows, value_rows, queries)],
        axis=2,
    )
    mine = lax.all_to_all(mine, "head", split_axis=0, concat_axis=0, tiled=True)
    mine = mine.reshape(SLOTS, 3 * WIDE)
    query = mine[:, 2 * WIDE :]
    own = lax.all_to_all(
        jnp.broadcast_to(mine[None, :, : 2 * WIDE], (SETS, SLOTS, 2 * WIDE)),
        ("x", "yl"),
        split_axis=0,
        concat_axis=0,
        tiled=True,
    )
    sent = [
        lax.ppermute(query, "yh", [(i, (i + k) % BANDS) for i in range(BANDS)])
        for k in ORDER[1:]
    ]
    bias = jax.ShapeDtypeStruct((2 * BANDS, SETS * SLOTS), jnp.float32)
    prepared = pl.pallas_call(
        prepare,
        out_shape=[bias] + [jax.ShapeDtypeStruct(latent.shape, jnp.float32)] * 2,
        in_specs=[smem] * 4 + [vmem] * 4,
        out_specs=[vmem] * 3,
        compiler_params=LIMIT,
    )(time_index, lengths, step_size, noise_level, visible, latent, fresh_noise, time_gate)
    bias, base, slope = prepared
    halves = [
        lax.all_gather(a.reshape(-1, 2 * WIDE), "core", axis=0, tiled=True)
        for a in (own[:BANDS], own[BANDS:])
    ]
    partial = pl.pallas_call(
        attend,
        out_shape=jax.ShapeDtypeStruct((BANDS, SLOTS, WIDE + HD), jnp.bfloat16),
        in_specs=[vmem] * (BANDS + 3),
        out_specs=vmem,
        compiler_params=LIMIT,
    )(query, *sent, *halves, bias)
    partial = lax.all_to_all(
        partial.reshape(BANDS * SETS, ROWS, WIDE + HD),
        ("yh", "head"),
        split_axis=0,
        concat_axis=0,
        tiled=True,
    )
    return pl.pallas_call(
        update,
        out_shape=jax.ShapeDtypeStruct(latent.shape, jnp.float32),
        in_specs=[vmem] * 3,
        out_specs=vmem,
        compiler_params=LIMIT,
    )(partial, base, slope)


def solution(mesh):
    names = ("yh", "yl", "x", "core", "head")
    grid = Mesh(mesh.devices.reshape(BANDS, 2, 4, 2, 8), names)
    tokens = P(names, None)
    placed = (tokens,) * 5 + (P(),) * 6
    return jax.shard_map(local, mesh=grid, in_specs=placed, out_specs=tokens, check_vma=False)
```
